32 devices in a mesh: seq: 16 (over z, y, x), ffn: 2 (over core).
Axes of the slice: x: 2, y: 2, z: 4, core: 2. Of those that a mesh axis runs over, the one named last changes fastest.
Arguments:
- patches: bfloat16 [4096, 4096], P('seq'), may hold values from -100 to 100
- gate_weight: bfloat16 [4096, 7168], P('seq', 'ffn'), may hold values from -0.09375 to 0.09375
- up_weight: bfloat16 [4096, 7168], P('seq', 'ffn'), may hold values from -0.09375 to 0.09375
- down_weight: bfloat16 [4096, 7168], P('seq', 'ffn'), may hold values from -0.25 to 0.25
- key_weight: bfloat16 [4096, 1024], P(None, 'ffn'), may hold values from -0.09375 to 0.09375
- value_weight: bfloat16 [4096, 1024], P(None, 'ffn'), may hold values from -0.09375 to 0.09375
- byte_states: bfloat16 [32768, 1024], P('seq'), may hold values from -60 to 60
- byte_patch: int32 [32768], P('seq'), may hold values from 0 to 4095, as said below
- cross_query: bfloat16 [1024, 1024], P(None, 'ffn'), may hold values from -0.375 to 0.375
- self_query: bfloat16 [1024, 1024], P(None, 'ffn'), may hold values from -0.375 to 0.375
- self_key: bfloat16 [1024, 1024], P(None, 'ffn'), may hold values from -0.375 to 0.375
- self_value: bfloat16 [1024, 1024], P(None, 'ffn'), may hold values from -0.1875 to 0.1875
- cross_out: bfloat16 [1024, 1024], P('ffn'), may hold values from -0.1875 to 0.1875
- self_out: bfloat16 [1024, 1024], P('ffn'), may hold values from -0.1875 to 0.1875
Outputs:
- update: bfloat16 [32768, 1024], P('seq', 'ffn')
The draws below stay inside these ranges and needn't reach their ends.
Inputs may be any that keep to these rules, and one draw needn't show every extreme that they name: byte_patch starts at 0, never falls, rises by at most 1 from one byte to the next and ends at 4095, so every patch is a run of one or more bytes. The bytes s * 2048 to (s + 1) * 2048 - 1 read only patches s * 256 - 23 to (s + 1) * 256 + 15; both ends are reached in every draw.
All inputs are finite; a program needn't handle non-finite values.
Results may differ from the reference program's by a relative error of at most 0.0085.
The reference program's roundings to bfloat16 on the way (of `normed`, `hidden`, `global_out`, `weights_c`, `context_c`, `weights_s` and `context_s`) count: a program that leaves them out, or rounds other values in their place, can miss the bound.
Values may be sent and summed in bfloat16 or wider, within the bound.
A program may use at most 192 MiB of HBM per device.

```python
import math
import jax
import jax.numpy as jnp
from jax import lax

D = 4096
FFW = 7168
DL = 1024
HD = 64
HEADS = 16
PWIN = 8
WINDOW = 512
DRIFT = 16
P_DEV = 256
B_DEV = 2048
NPATCH = 4096
NBYTES = 32768
N_SEQ = 16


def draw_patches(key, part):
    key_rows, key_cols, key_base = jax.random.split(jax.random.fold_in(key, 5), 3)
    row_scale = jnp.exp(jax.random.uniform(key_rows, (NPATCH, 1), minval=math.log(0.5), maxval=math.log(5.0)))
    col_scale = jnp.exp(jax.random.uniform(key_cols, (1, D), minval=math.log(0.2), maxval=math.log(2.0)))
    values = jnp.clip(jax.random.normal(key_base, (NPATCH, D)), -4.0, 4.0)
    return jnp.clip(values * row_scale * col_scale, -100.0, 100.0).astype(jnp.bfloat16)


def draw_byte_states(key, part):
    key_rows, key_base = jax.random.split(jax.random.fold_in(key, 7), 2)
    row_scale = jnp.exp(jax.random.uniform(key_rows, (NBYTES, 1), minval=math.log(0.5), maxval=math.log(2.0)))
    values = jnp.clip(jax.random.normal(key_base, (NBYTES, DL)), -4.0, 4.0)
    return jnp.clip(values * row_scale, -60.0, 60.0).astype(jnp.bfloat16)


def draw_byte_patch(key, part):
    key_drift, key_pick, key_score = jax.random.split(jax.random.fold_in(key, 17), 3)
    shifts = jax.random.randint(key_drift, (N_SEQ + 1,), -DRIFT, DRIFT + 1)
    chosen = jax.random.permutation(key_pick, N_SEQ - 1)[:2] + 1
    slab_ids = jnp.arange(N_SEQ + 1, dtype=jnp.int32)
    shifts = jnp.where(slab_ids == chosen[0], -DRIFT, shifts)
    shifts = jnp.where(slab_ids == chosen[1], DRIFT, shifts)
    shifts = jnp.where((slab_ids == 0) | (slab_ids == N_SEQ), 0, shifts)
    slab_start = slab_ids * B_DEV + shifts
    lengths = slab_start[1:] - slab_start[:-1]
    longest = B_DEV + 2 * DRIFT
    places = jnp.arange(1, longest, dtype=jnp.int32)
    limit = 1073741824 // longest
    scores = jax.random.randint(key_score, (N_SEQ, longest - 1), 0, limit) * longest + places[None, :]
    slab_rows = jnp.arange(N_SEQ, dtype=jnp.int32)[:, None]
    forced_low = (slab_rows == chosen[0]) & (places[None, :] <= DRIFT)
    forced_high = (slab_rows + 1 == chosen[1]) & (places[None, :] >= lengths[:, None] - DRIFT)
    scores = jnp.where(forced_low | forced_high, 1073741824 + places[None, :], scores)
    scores = jnp.where(places[None, :] < lengths[:, None], scores, -places[None, :])
    picked = lax.top_k(scores, P_DEV - 1)[1].astype(jnp.int32) + 1
    cuts = jnp.sort(picked, axis=1)
    starts = jnp.concatenate([jnp.zeros((N_SEQ, 1), jnp.int32), cuts], axis=1) + slab_start[:N_SEQ, None]
    positions = jnp.arange(NBYTES, dtype=jnp.int32)
    found = jnp.searchsorted(starts.reshape(-1), positions, side='right')
    return (found - 1).astype(jnp.int32)


def steps_of(stream_key, shape, shards, least, largest):
    loudness, own = 1.0, jax.random.fold_in(stream_key, 6)
    for axis_at, parts in shards:
        heights = jnp.exp(jax.random.uniform(jax.random.fold_in(own, axis_at), (parts,), jnp.float32, least / len(shards), largest / len(shards)))
        loudness = loudness * jnp.repeat(heights, shape[axis_at] // parts).reshape([-1 if axis == axis_at else 1 for axis in range(len(shape))])
    return loudness


def noise(stream_key, extent, deviation, most, pieces=(), kind=jnp.bfloat16):
    factor_of = steps_of(stream_key, extent, pieces, -0.22, 0.18) if pieces else 1.0
    drawn = jax.random.normal(stream_key, extent, jnp.float32) * deviation * factor_of
    return jnp.minimum(jnp.maximum(drawn, -most), most).astype(kind)


def setup_inputs(seed: int = 0) -> dict:
    seeds = jax.random.split(jax.random.key(seed), 15)
    patches = draw_patches(jax.random.fold_in(seeds[14], 71), 0)
    gate_weight = noise(seeds[1], (D, FFW), D ** -0.5, 0.09375, ((0, 16), (1, 2)))
    up_weight = noise(seeds[2], (D, FFW), D ** -0.5, 0.09375, ((0, 16), (1, 2)))
    down_weight = noise(seeds[3], (D, FFW), (FFW // 16) ** -0.5, 0.25, ((0, 16), (1, 2)))
    key_weight = noise(seeds[4], (D, DL), D ** -0.5, 0.09375, ((1, 2),))
    value_weight = noise(seeds[5], (D, DL), D ** -0.5, 0.09375, ((1, 2),))
    byte_states = draw_byte_states(jax.random.fold_in(seeds[14], 71), 0)
    byte_patch = draw_byte_patch(jax.random.fold_in(seeds[14], 71), 0)
    cross_query = noise(seeds[8], (DL, DL), (DL // 4) ** -0.5, 0.375, ((1, 2),))
    self_query = noise(seeds[9], (DL, DL), (DL // 4) ** -0.5, 0.375, ((1, 2),))
    self_key = noise(seeds[10], (DL, DL), (DL // 4) ** -0.5, 0.375, ((1, 2),))
    self_value = noise(seeds[11], (DL, DL), DL ** -0.5, 0.1875, ((1, 2),))
    cross_out = noise(seeds[12], (DL, DL), DL ** -0.5, 0.1875, ((0, 2),))
    self_out = noise(seeds[13], (DL, DL), DL ** -0.5, 0.1875, ((0, 2),))
    return {"patches": patches, "gate_weight": gate_weight, "up_weight": up_weight, "down_weight": down_weight, "key_weight": key_weight, "value_weight": value_weight, "byte_states": byte_states, "byte_patch": byte_patch, "cross_query": cross_query, "self_query": self_query, "self_key": self_key, "self_value": self_value, "cross_out": cross_out, "self_out": self_out}


EPS = 1e-05

def row_normalize(matrix):
    widened = matrix.astype(jnp.float32)
    return widened * lax.rsqrt(lax.optimization_barrier(jnp.mean(widened * widened, axis=-1, keepdims=True)) + EPS)

def masked_softmax(scores, key_mask):
    masked = jnp.where(key_mask, scores, -jnp.inf)
    row_max = lax.optimization_barrier(jnp.max(masked, axis=-1, keepdims=True))
    exp_terms = jnp.exp(masked - row_max)
    return exp_terms / lax.optimization_barrier(jnp.sum(exp_terms, axis=-1, keepdims=True))

def reference(patches, gate_weight, up_weight, down_weight, key_weight, value_weight, byte_states, byte_patch, cross_query, self_query, self_key, self_value, cross_out, self_out):
    normed = row_normalize(patches).astype(jnp.bfloat16)
    gate_sum = jnp.dot(normed, gate_weight, preferred_element_type=jnp.float32)
    up_sum = jnp.dot(normed, up_weight, preferred_element_type=jnp.float32)
    hidden = (jax.nn.silu(gate_sum) * up_sum).astype(jnp.bfloat16)
    ffn_out = lax.dot_general(hidden, down_weight, (((1,), (1,)), ((), ())), preferred_element_type=jnp.float32)
    global_out = (patches.astype(jnp.float32) + ffn_out).astype(jnp.bfloat16)
    keys_c = jnp.dot(global_out, key_weight, preferred_element_type=jnp.float32).astype(jnp.bfloat16)
    values_c = jnp.dot(global_out, value_weight, preferred_element_type=jnp.float32).astype(jnp.bfloat16)
    query_c = jnp.dot(byte_states, cross_query, preferred_element_type=jnp.float32).astype(jnp.bfloat16)
    query_s = jnp.dot(byte_states, self_query, preferred_element_type=jnp.float32).astype(jnp.bfloat16)
    keys_s = jnp.dot(byte_states, self_key, preferred_element_type=jnp.float32).astype(jnp.bfloat16)
    values_s = jnp.dot(byte_states, self_value, preferred_element_type=jnp.float32).astype(jnp.bfloat16)
    score_scale = 1.0 / math.sqrt(HD)
    key_span = WINDOW + PWIN
    blocks = NBYTES // WINDOW

    def cross_block(block_id):
        offset = (block_id * WINDOW).astype(jnp.int32)
        query_block = lax.dynamic_slice_in_dim(query_c, offset, WINDOW, 0).astype(jnp.float32).reshape(WINDOW, HEADS, HD)
        patch_block = lax.dynamic_slice_in_dim(byte_patch, offset, WINDOW, 0)
        first_key = jnp.clip(patch_block[0] - PWIN + 1, 0, NPATCH - key_span).astype(jnp.int32)
        key_block = lax.dynamic_slice_in_dim(keys_c, first_key, key_span, 0).astype(jnp.float32).reshape(key_span, HEADS, HD)
        value_block = lax.dynamic_slice_in_dim(values_c, first_key, key_span, 0).astype(jnp.float32).reshape(key_span, HEADS, HD)
        key_index = first_key + jnp.arange(key_span, dtype=jnp.int32)
        key_mask = (key_index[None, :] <= patch_block[:, None]) & (key_index[None, :] > patch_block[:, None] - PWIN)
        scores = jnp.einsum('qhd,khd->hqk', query_block, key_block) * score_scale
        weights_c = masked_softmax(scores, key_mask[None]).astype(jnp.bfloat16)
        context = jnp.einsum('hqk,khd->qhd', weights_c.astype(jnp.float32), value_block)
        return context.astype(jnp.bfloat16).reshape(WINDOW, DL)
    context_c = lax.map(cross_block, jnp.arange(blocks, dtype=jnp.int32)).reshape(NBYTES, DL)
    keys_padded = jnp.concatenate([jnp.zeros((WINDOW, DL), jnp.bfloat16), keys_s], axis=0)
    values_padded = jnp.concatenate([jnp.zeros((WINDOW, DL), jnp.bfloat16), values_s], axis=0)

    def self_block(block_id):
        offset = (block_id * WINDOW).astype(jnp.int32)
        query_block = lax.dynamic_slice_in_dim(query_s, offset, WINDOW, 0).astype(jnp.float32).reshape(WINDOW, HEADS, HD)
        key_block = lax.dynamic_slice_in_dim(keys_padded, offset, 2 * WINDOW, 0).astype(jnp.float32).reshape(2 * WINDOW, HEADS, HD)
        value_block = lax.dynamic_slice_in_dim(values_padded, offset, 2 * WINDOW, 0).astype(jnp.float32).reshape(2 * WINDOW, HEADS, HD)
        query_pos = offset + jnp.arange(WINDOW, dtype=jnp.int32)
        key_pos = offset - WINDOW + jnp.arange(2 * WINDOW, dtype=jnp.int32)
        key_mask = (key_pos[None, :] <= query_pos[:, None]) & (key_pos[None, :] > query_pos[:, None] - WINDOW) & (key_pos[None, :] >= 0)
        scores = jnp.einsum('qhd,khd->hqk', query_block, key_block) * score_scale
        weights_s = masked_softmax(scores, key_mask[None]).astype(jnp.bfloat16)
        context = jnp.einsum('hqk,khd->qhd', weights_s.astype(jnp.float32), value_block)
        return context.astype(jnp.bfloat16).reshape(WINDOW, DL)
    context_s = lax.map(self_block, jnp.arange(blocks, dtype=jnp.int32)).reshape(NBYTES, DL)
    update = jnp.dot(context_c, cross_out, preferred_element_type=jnp.float32) + jnp.dot(context_s, self_out, preferred_element_type=jnp.float32)
    return update.astype(jnp.bfloat16)
```

```python
import math

import jax
import jax.numpy as jnp
from jax import lax
from jax.sharding import PartitionSpec as P

HD = 64
PWIN = 8
WINDOW = 512
HALO = 23
GROUP = 4


EPS = 1e-05


def padded(value, sides, width):
    for axis, dim in sides:
        count, length = (lax.axis_size(axis), value.shape[dim])
        up = [(i, (i + 1) % count) for i in range(count - 1)]
        down = [(j, i) for i, j in up]
        last = lax.slice_in_dim(value, length - width, length, axis=dim)
        first = lax.slice_in_dim(value, 0, width, axis=dim)
        before = lax.ppermute(last, axis, up)
        after = lax.ppermute(first, axis, down)
        value = jnp.concatenate([before, value, after], axis=dim)
    return value


def along_far(value, by):
    if by == 0:
        return value
    count = lax.axis_size("seq")
    plane = count // GROUP
    pairs = [(i, ((i // plane) ^ by) * plane + i % plane) for i in range(count)]
    return lax.ppermute(value, "seq", pairs)


def along_near(value, by):
    if by == 0:
        return value
    return lax.ppermute(value, "seq", [(i, i ^ by) for i in range(lax.axis_size("seq"))])


def along_ffn(value, by):
    if by == 0:
        return value
    return lax.ppermute(value, "ffn", [(i, i ^ by) for i in range(lax.axis_size("ffn"))])


def shifted(value, axis, by):
    count = lax.axis_size(axis)
    pairs = [(i, i + by) for i in range(count) if 0 <= i + by < count]
    return lax.ppermute(value, axis, pairs)


def row_normalize(matrix):
    widened = matrix.astype(jnp.float32)
    return widened * lax.rsqrt(jnp.mean(widened * widened, axis=-1, keepdims=True) + EPS)


def masked_softmax(scores, key_mask):
    masked = jnp.where(key_mask, scores, -jnp.inf)
    row_max = jnp.max(masked, axis=-1, keepdims=True)
    exp_terms = jnp.exp(masked - row_max)
    return exp_terms / jnp.sum(exp_terms, axis=-1, keepdims=True)


def local(
    patches,
    gate_weight,
    up_weight,
    down_weight,
    key_weight,
    value_weight,
    byte_states,
    byte_patch,
    cross_query,
    self_query,
    self_key,
    self_value,
    cross_out,
    self_out,
):
    patch_count, width = patches.shape
    rows, units = gate_weight.shape
    ring = lax.axis_size("seq")
    plane = ring // GROUP
    cores = lax.axis_size("ffn")
    seq_at = lax.axis_index("seq")
    core_at = lax.axis_index("ffn")
    far, near = seq_at // plane, seq_at % plane

    share = width // cores
    mine = lax.dynamic_slice_in_dim(patches, core_at * share, share, axis=1)
    held = jnp.zeros((GROUP * patch_count, share), patches.dtype)
    for k in range(GROUP):
        held = lax.dynamic_update_slice_in_dim(
            held, along_far(mine, k), (far ^ k) * patch_count, axis=0
        )
    group = jnp.zeros((GROUP * patch_count, width), patches.dtype)
    for k in range(cores):
        group = lax.dynamic_update_slice_in_dim(
            group, along_ffn(held, k), (core_at ^ k) * share, axis=1
        )
    normed = row_normalize(group).astype(jnp.bfloat16)
    slabs = []
    for j in range(plane):
        picked = [
            lax.dynamic_slice_in_dim(normed, ((far ^ k) * plane + (near ^ j)) * rows, rows, axis=1)
            for k in range(GROUP)
        ]
        slabs.append(jnp.concatenate(picked, axis=1))

    quarter = units // GROUP
    head = min(quarter, -(-quarter // 256) * 128)
    pieces = [(0, head), (head, quarter - head)]
    hidden_all = jnp.zeros((GROUP * patch_count, units), jnp.bfloat16)
    for at, size in pieces:
        column = []
        for k in range(GROUP):
            start = (far ^ k) * quarter + at
            both = jnp.concatenate(
                [
                    lax.dynamic_slice_in_dim(gate_weight, start, size, axis=1),
                    lax.dynamic_slice_in_dim(up_weight, start, size, axis=1),
                ],
                axis=1,
            )
            column.append(along_far(both, k))
        column = jnp.concatenate(column, axis=0)
        sums = 0.0
        for j in range(plane):
            sums += jnp.dot(
                slabs[j], along_near(column, j), preferred_element_type=jnp.float32
            )
        hidden = (jax.nn.silu(sums[:, :size]) * sums[:, size:]).astype(jnp.bfloat16)
        for k in range(GROUP):
            hidden_all = lax.dynamic_update_slice_in_dim(
                hidden_all, along_far(hidden, k), (far ^ k) * quarter + at, axis=1
            )

    down = jnp.zeros((plane * rows, units), down_weight.dtype)
    for j in range(plane):
        down = lax.dynamic_update_slice_in_dim(
            down, along_near(down_weight, j), (near ^ j) * rows, axis=0
        )
    ffn_out = lax.dot_general(
        hidden_all, down, (((1,), (1,)), ((), ())), preferred_element_type=jnp.float32
    )
    cut = plane * rows // cores
    ffn_whole = 0.0
    for k in range(cores):
        ffn_whole += along_ffn(
            lax.dynamic_slice_in_dim(ffn_out, (core_at ^ k) * cut, cut, axis=1), k
        )
    group_cut = lax.dynamic_slice_in_dim(group, (far * cores + core_at) * cut, cut, axis=1)
    out_cut = (group_cut.astype(jnp.float32) + ffn_whole).astype(jnp.bfloat16)
    returned = jnp.concatenate(
        [
            along_far(
                lax.dynamic_slice_in_dim(out_cut, (far ^ k) * patch_count, patch_count, axis=0), k
            )
            for k in range(GROUP)
        ],
        axis=1,
    )
    global_out = jnp.zeros((patch_count, width), jnp.bfloat16)
    for c in range(cores):
        other = along_ffn(returned, c)
        for k in range(GROUP):
            global_out = lax.dynamic_update_slice_in_dim(
                global_out,
                other[:, k * cut : (k + 1) * cut],
                ((far ^ k) * cores + (core_at ^ c)) * cut,
                axis=1,
            )
    head_cols = key_weight.shape[1]
    head_count = head_cols // HD
    score_scale = 1.0 / math.sqrt(HD)
    seq_index = lax.axis_index("seq")
    keys_c = jnp.dot(global_out, key_weight, preferred_element_type=jnp.float32).astype(
        jnp.bfloat16
    )
    values_c = jnp.dot(global_out, value_weight, preferred_element_type=jnp.float32).astype(
        jnp.bfloat16
    )
    both_c = jnp.concatenate([keys_c, values_c], axis=1)
    extended = padded(both_c, (("seq", 0),), HALO)
    key_count = extended.shape[0]
    key_index = seq_index * patch_count - HALO + jnp.arange(key_count, dtype=jnp.int32)
    cross_mask = (
        (key_index[None, :] <= byte_patch[:, None])
        & (key_index[None, :] > byte_patch[:, None] - PWIN)
        & (key_index[None, :] >= 0)
    )
    byte_count = byte_states.shape[0]
    query_c = jnp.dot(byte_states, cross_query, preferred_element_type=jnp.float32).astype(
        jnp.bfloat16
    )
    query_s = jnp.dot(byte_states, self_query, preferred_element_type=jnp.float32).astype(
        jnp.bfloat16
    )
    keys_s = jnp.dot(byte_states, self_key, preferred_element_type=jnp.float32).astype(jnp.bfloat16)
    values_s = jnp.dot(byte_states, self_value, preferred_element_type=jnp.float32).astype(
        jnp.bfloat16
    )
    query_here = query_c.reshape(byte_count, head_count, HD)
    keys_here = extended[:, :head_cols].reshape(key_count, head_count, HD)
    values_here = extended[:, head_cols:].reshape(key_count, head_count, HD)
    cross_scores = (
        jnp.einsum("qhd,khd->hqk", query_here, keys_here, preferred_element_type=jnp.float32)
        * score_scale
    )
    weights_c = masked_softmax(cross_scores, cross_mask[None]).astype(jnp.bfloat16)
    context_c = jnp.einsum(
        "hqk,khd->qhd", weights_c, values_here, preferred_element_type=jnp.float32
    )
    context_c = context_c.astype(jnp.bfloat16).reshape(byte_count, head_cols)
    both_s = jnp.concatenate([keys_s, values_s], axis=1)
    tail_rows = both_s[byte_count - WINDOW :]
    before = shifted(tail_rows, "seq", 1)
    stacked = jnp.concatenate([before, both_s], axis=0)
    blocks = byte_count // WINDOW
    lower_half = stacked[:byte_count].reshape(blocks, WINDOW, 2 * head_cols)
    upper_half = stacked[WINDOW:].reshape(blocks, WINDOW, 2 * head_cols)
    key_pairs = jnp.concatenate([lower_half, upper_half], axis=1)
    window_keys = key_pairs[:, :, :head_cols].reshape(blocks, 2 * WINDOW, head_count, HD)
    window_values = key_pairs[:, :, head_cols:].reshape(blocks, 2 * WINDOW, head_count, HD)
    window_queries = query_s.reshape(blocks, WINDOW, head_count, HD)
    self_scores = (
        jnp.einsum(
            "bqhd,bkhd->bhqk", window_queries, window_keys, preferred_element_type=jnp.float32
        )
        * score_scale
    )
    query_slot = jnp.arange(WINDOW, dtype=jnp.int32)[:, None]
    key_slot = jnp.arange(2 * WINDOW, dtype=jnp.int32)[None, :]
    band_mask = (key_slot > query_slot) & (key_slot <= query_slot + WINDOW)
    block_ids = jnp.arange(blocks, dtype=jnp.int32)
    key_pos = (
        seq_index * byte_count
        - WINDOW
        + block_ids[:, None] * WINDOW
        + jnp.arange(2 * WINDOW, dtype=jnp.int32)[None, :]
    )
    self_mask = band_mask[None, None] & (key_pos >= 0)[:, None, None, :]
    weights_s = masked_softmax(self_scores, self_mask).astype(jnp.bfloat16)
    context_s = jnp.einsum(
        "bhqk,bkhd->bqhd", weights_s, window_values, preferred_element_type=jnp.float32
    )
    context_s = context_s.astype(jnp.bfloat16).reshape(byte_count, head_cols)
    out_cols = cross_out.shape[1] // cores
    total = 0.0
    for context, weight in ((context_s, self_out), (context_c, cross_out)):
        for k in range(cores):
            block = lax.dynamic_slice_in_dim(weight, (core_at ^ k) * out_cols, out_cols, axis=1)
            total += jnp.dot(
                along_ffn(context, k), along_ffn(block, k), preferred_element_type=jnp.float32
            )
    return total.astype(jnp.bfloat16)


def solution(mesh):
    placed = (
        P("seq", None),
        P("seq", "ffn"),
        P("seq", "ffn"),
        P("seq", "ffn"),
        P(None, "ffn"),
        P(None, "ffn"),
        P("seq", None),
        P("seq"),
        P(None, "ffn"),
        P(None, "ffn"),
        P(None, "ffn"),
        P(None, "ffn"),
        P("ffn", None),
        P("ffn", None),
    )
    return jax.shard_map(
        local, mesh=mesh, in_specs=placed, out_specs=P("seq", "ffn"), check_vma=False
    )
```

```python
import math

import jax
import jax.numpy as jnp
from jax import lax
from jax.experimental import pallas as pl
from jax.experimental.pallas import tpu as pltpu
from jax.sharding import PartitionSpec as P

HD = 64
PWIN = 8
WINDOW = 512
HALO = 23
GROUP = 4


EPS = 1e-05


def padded(value, sides, width):
    for axis, dim in sides:
        count, length = (lax.axis_size(axis), value.shape[dim])
        up = [(i, (i + 1) % count) for i in range(count - 1)]
        down = [(j, i) for i, j in up]
        last = lax.slice_in_dim(value, length - width, length, axis=dim)
        first = lax.slice_in_dim(value, 0, width, axis=dim)
        before = lax.ppermute(last, axis, up)
        after = lax.ppermute(first, axis, down)
        value = jnp.concatenate([before, value, after], axis=dim)
    return value


def along_far(value, by):
    if by == 0:
        return value
    count = lax.axis_size("seq")
    plane = count // GROUP
    pairs = [(i, ((i // plane) ^ by) * plane + i % plane) for i in range(count)]
    return lax.ppermute(value, "seq", pairs)


def along_near(value, by):
    if by == 0:
        return value
    return lax.ppermute(value, "seq", [(i, i ^ by) for i in range(lax.axis_size("seq"))])


def along_ffn(value, by):
    if by == 0:
        return value
    return lax.ppermute(value, "ffn", [(i, i ^ by) for i in range(lax.axis_size("ffn"))])


def shifted(value, axis, by):
    count = lax.axis_size(axis)
    pairs = [(i, i + by) for i in range(count) if 0 <= i + by < count]
    return lax.ppermute(value, axis, pairs)


def row_normalize(matrix):
    widened = matrix.astype(jnp.float32)
    return widened * lax.rsqrt(jnp.mean(widened * widened, axis=-1, keepdims=True) + EPS)


def masked_softmax(scores, key_mask):
    masked = jnp.where(key_mask, scores, -jnp.inf)
    row_max = jnp.max(masked, axis=-1, keepdims=True)
    exp_terms = jnp.exp(masked - row_max)
    return exp_terms / jnp.sum(exp_terms, axis=-1, keepdims=True)


def cross_kernel(query_ref, key_ref, value_ref, bounds_ref, out_ref):
    keys, count = key_ref.shape[0], query_ref.shape[1]
    slot = lax.broadcasted_iota(jnp.int32, (keys, count), 0)
    inside = (slot >= bounds_ref[0:1, :]) & (slot <= bounds_ref[1:2, :])
    bias = jnp.where(inside, 0.0, -jnp.inf)
    for head in range(query_ref.shape[0] // HD):
        part = slice(head * HD, (head + 1) * HD)
        scores = bias + jnp.dot(
            key_ref[:, part], query_ref[part, :], preferred_element_type=jnp.float32
        )
        terms = jnp.exp(scores - jnp.max(scores, axis=0, keepdims=True))
        weights = terms * (1.0 / jnp.sum(terms, axis=0, keepdims=True))
        out_ref[part, :] = jnp.dot(
            value_ref[part, :], weights.astype(jnp.bfloat16), preferred_element_type=jnp.float32
        ).astype(jnp.bfloat16)


def cross_attention(query, extended, first_slot, last_slot):
    columns, count = query.shape
    extended = jnp.pad(extended, ((0, -extended.shape[0] % 16), (0, 0)))
    keys = extended.shape[0]
    values = extended[:, columns:].T
    bounds = jnp.stack([first_slot, last_slot] + [last_slot] * 6)
    run = min(count, 512)
    return pl.pallas_call(
        cross_kernel,
        grid=(count // run,),
        in_specs=[
            pl.BlockSpec((columns, run), lambda i: (0, i)),
            pl.BlockSpec((keys, columns), lambda i: (0, 0)),
            pl.BlockSpec((columns, keys), lambda i: (0, 0)),
            pl.BlockSpec((8, run), lambda i: (0, i)),
        ],
        out_specs=pl.BlockSpec((columns, run), lambda i: (0, i)),
        out_shape=jax.ShapeDtypeStruct((columns, count), jnp.bfloat16),
        compiler_params=pltpu.CompilerParams(vmem_limit_bytes=32 * 1024 * 1024),
    )(query, extended[:, :columns], values, bounds)


def local(
    patches,
    gate_weight,
    up_weight,
    down_weight,
    key_weight,
    value_weight,
    byte_states,
    byte_patch,
    cross_query,
    self_query,
    self_key,
    self_value,
    cross_out,
    self_out,
):
    patch_count, width = patches.shape
    rows, units = gate_weight.shape
    ring = lax.axis_size("seq")
    plane = ring // GROUP
    cores = lax.axis_size("ffn")
    seq_at = lax.axis_index("seq")
    core_at = lax.axis_index("ffn")
    far, near = seq_at // plane, seq_at % plane

    head_cols = key_weight.shape[1]
    head_count = head_cols // HD
    score_scale = 1.0 / math.sqrt(HD)
    seq_index = lax.axis_index("seq")

    byte_count = byte_states.shape[0]
    out_cols = cross_out.shape[1] // cores

    def out_share(context, weight, depth_axis):
        total = 0.0
        for k in range(cores):
            block = lax.dynamic_slice_in_dim(weight, (core_at ^ k) * out_cols, out_cols, axis=1)
            total += lax.dot_general(
                along_ffn(context, k),
                along_ffn(block, k),
                (((depth_axis,), (0,)), ((), ())),
                preferred_element_type=jnp.float32,
            )
        return total

    query_s = jnp.dot(byte_states, self_query, preferred_element_type=jnp.float32).astype(
        jnp.bfloat16
    )
    keys_s = jnp.dot(byte_states, self_key, preferred_element_type=jnp.float32).astype(jnp.bfloat16)
    values_s = jnp.dot(byte_states, self_value, preferred_element_type=jnp.float32).astype(
        jnp.bfloat16
    )
    query_c = (
        lax.dot_general(
            cross_query, byte_states, (((0,), (1,)), ((), ())), preferred_element_type=jnp.float32
        )
        * score_scale
    ).astype(jnp.bfloat16)
    both_s = jnp.concatenate([keys_s, values_s], axis=1)
    tail_rows = both_s[byte_count - WINDOW :]
    before = shifted(tail_rows, "seq", 1)
    stacked = jnp.concatenate([before, both_s], axis=0)
    blocks = byte_count // WINDOW
    lower_half = stacked[:byte_count].reshape(blocks, WINDOW, 2 * head_cols)
    upper_half = stacked[WINDOW:].reshape(blocks, WINDOW, 2 * head_cols)
    key_pairs = jnp.concatenate([lower_half, upper_half], axis=1)
    window_keys = key_pairs[:, :, :head_cols].reshape(blocks, 2 * WINDOW, head_count, HD)
    window_values = key_pairs[:, :, head_cols:].reshape(blocks, 2 * WINDOW, head_count, HD)
    window_queries = query_s.reshape(blocks, WINDOW, head_count, HD)
    self_scores = (
        jnp.einsum(
            "bqhd,bkhd->bhqk", window_queries, window_keys, preferred_element_type=jnp.float32
        )
        * score_scale
    )
    query_slot = jnp.arange(WINDOW, dtype=jnp.int32)[:, None]
    key_slot = jnp.arange(2 * WINDOW, dtype=jnp.int32)[None, :]
    band_mask = (key_slot > query_slot) & (key_slot <= query_slot + WINDOW)
    block_ids = jnp.arange(blocks, dtype=jnp.int32)
    key_pos = (
        seq_index * byte_count
        - WINDOW
        + block_ids[:, None] * WINDOW
        + jnp.arange(2 * WINDOW, dtype=jnp.int32)[None, :]
    )
    self_mask = band_mask[None, None] & (key_pos >= 0)[:, None, None, :]
    weights_s = masked_softmax(self_scores, self_mask).astype(jnp.bfloat16)
    context_s = jnp.einsum(
        "bhqk,bkhd->bqhd", weights_s, window_values, preferred_element_type=jnp.float32
    )
    context_s = context_s.astype(jnp.bfloat16).reshape(byte_count, head_cols)

    quarter = units // GROUP
    head = min(quarter, -(-quarter // 256) * 128)
    pieces = [(0, head), (head, quarter - head)]

    def fetch_column(gate, up, at, size):
        column = []
        for k in range(GROUP):
            start = (far ^ k) * quarter + at
            both = jnp.concatenate(
                [
                    lax.dynamic_slice_in_dim(gate, start, size, axis=1),
                    lax.dynamic_slice_in_dim(up, start, size, axis=1),
                ],
                axis=1,
            )
            column.append(along_far(both, k))
        return jnp.concatenate(column, axis=0)

    columns = [fetch_column(gate_weight, up_weight, *pieces[0])]
    columns[0], patches, gate_weight, up_weight = lax.optimization_barrier(
        (columns[0], patches, gate_weight, up_weight)
    )
    columns.append(fetch_column(gate_weight, up_weight, *pieces[1]))
    down_blocks = [along_near(down_weight, j) for j in range(plane - 1)]

    share = width // cores
    mine = lax.dynamic_slice_in_dim(patches, core_at * share, share, axis=1)
    held = jnp.zeros((GROUP * patch_count, share), patches.dtype)
    for k in range(GROUP):
        held = lax.dynamic_update_slice_in_dim(
            held, along_far(mine, k), (far ^ k) * patch_count, axis=0
        )
    group = jnp.zeros((GROUP * patch_count, width), patches.dtype)
    for k in range(cores):
        group = lax.dynamic_update_slice_in_dim(
            group, along_ffn(held, k), (core_at ^ k) * share, axis=1
        )
    normed = row_normalize(group).astype(jnp.bfloat16)
    slabs = []
    for j in range(plane):
        picked = [
            lax.dynamic_slice_in_dim(normed, ((far ^ k) * plane + (near ^ j)) * rows, rows, axis=1)
            for k in range(GROUP)
        ]
        slabs.append(jnp.concatenate(picked, axis=1))

    slabs, context_s = lax.optimization_barrier((slabs, context_s))
    gathered = [[along_near(column, j) for j in range(plane)] for column in columns]
    gathered[1], down_weight = lax.optimization_barrier((gathered[1], down_weight))
    down_blocks.append(along_near(down_weight, plane - 1))

    hidden_all = jnp.zeros((GROUP * patch_count, units), jnp.bfloat16)
    for (at, size), blocks_here in zip(pieces, gathered):
        sums = 0.0
        for j in range(plane):
            sums += jnp.dot(slabs[j], blocks_here[j], preferred_element_type=jnp.float32)
        hidden = (jax.nn.silu(sums[:, :size]) * sums[:, size:]).astype(jnp.bfloat16)
        for k in range(GROUP):
            hidden_all = lax.dynamic_update_slice_in_dim(
                hidden_all, along_far(hidden, k), (far ^ k) * quarter + at, axis=1
            )

    total_s = out_share(context_s, self_out, 1)
    hidden_all, total_s, query_c = lax.optimization_barrier((hidden_all, total_s, query_c))
    down = jnp.zeros((plane * rows, units), down_weight.dtype)
    for j in range(plane):
        down = lax.dynamic_update_slice_in_dim(
            down, down_blocks[j], (near ^ j) * rows, axis=0
        )
    ffn_out = lax.dot_general(
        hidden_all, down, (((1,), (1,)), ((), ())), preferred_element_type=jnp.float32
    )
    cut = plane * rows // cores
    ffn_whole = 0.0
    for k in range(cores):
        ffn_whole += along_ffn(
            lax.dynamic_slice_in_dim(ffn_out, (core_at ^ k) * cut, cut, axis=1), k
        )
    group_cut = lax.dynamic_slice_in_dim(group, (far * cores + core_at) * cut, cut, axis=1)
    out_cut = (group_cut.astype(jnp.float32) + ffn_whole).astype(jnp.bfloat16)
    returned = jnp.concatenate(
        [
            along_far(
                lax.dynamic_slice_in_dim(out_cut, (far ^ k) * patch_count, patch_count, axis=0), k
            )
            for k in range(GROUP)
        ],
        axis=1,
    )
    global_out = jnp.zeros((patch_count, width), jnp.bfloat16)
    for c in range(cores):
        other = along_ffn(returned, c)
        for k in range(GROUP):
            global_out = lax.dynamic_update_slice_in_dim(
                global_out,
                other[:, k * cut : (k + 1) * cut],
                ((far ^ k) * cores + (core_at ^ c)) * cut,
                axis=1,
            )
    keys_c = jnp.dot(global_out, key_weight, preferred_element_type=jnp.float32).astype(
        jnp.bfloat16
    )
    values_c = jnp.dot(global_out, value_weight, preferred_element_type=jnp.float32).astype(
        jnp.bfloat16
    )
    both_c = jnp.concatenate([keys_c, values_c], axis=1)
    extended = padded(both_c, (("seq", 0),), HALO)
    first_key = seq_index * patch_count - HALO
    last_slot = byte_patch - first_key
    first_slot = jnp.maximum(last_slot - (PWIN - 1), -first_key)
    context_c = cross_attention(query_c, extended, first_slot, last_slot)
    total = total_s + out_share(context_c, cross_out, 0)
    return total.astype(jnp.bfloat16)


def solution(mesh):
    placed = (
        P("seq", None),
        P("seq", "ffn"),
        P("seq", "ffn"),
        P("seq", "ffn"),
        P(None, "ffn"),
        P(None, "ffn"),
        P("seq", None),
        P("seq"),
        P(None, "ffn"),
        P(None, "ffn"),
        P(None, "ffn"),
        P(None, "ffn"),
        P("ffn", None),
        P("ffn", None),
    )
    return jax.shard_map(
        local, mesh=mesh, in_specs=placed, out_specs=P("seq", "ffn"), check_vma=False
    )
```
